32 devices in a mesh: grp: 4 (over y, core), mem: 8 (over z, x).
Axes of the slice: x: 2, y: 2, z: 4, core: 2. Of those that a mesh axis runs over, the one named last changes fastest.
Arguments:
- vectors: bfloat16 [32768, 768], P(('grp', 'mem')), may hold values from -6 to 6
- parents: int32 [32768], P(('grp', 'mem')), may hold values from 0 to 1
- children: int32 [32768], P(('grp', 'mem')), may hold values from 0 to 1023
- counts: int32 [32, 4], P(('grp', 'mem')), may hold values from 85 to 512, as said below
Outputs:
- distances: float32 [65536, 1024], P(('grp', 'mem'))
The draws below stay inside these ranges and needn't reach their ends.
Inputs may be any that keep to these rules, and one draw needn't show every extreme that they name: Each row of counts sums to 1024; shard d's vectors go to group 0 first, then group 1, and so on, in that many rows each. In every draw some group receives 512 vectors from every storage shard.
All inputs are finite; a program needn't handle non-finite values.
Results may differ from the reference program's by a relative error of at most 0.00055.
Values may be sent and summed in bfloat16 or wider, within the bound.
A program may use at most 128 MiB of HBM per device.

```python
import math
import jax
import jax.numpy as jnp
import numpy as np
from jax import lax

D = 768
CHILD = 1024
PAR_GRP = 2
VEC_DEV = 1024
GROUPS = 4
STORES = 32
SHARD_GROUP_SLOTS = 512
ROWS = 32768
N_GRP = 4
N_MEM = 8


def draw_counts(key, part):
    heavy_key, weight_key = jax.random.split(jax.random.fold_in(key, 11), 2)
    heavy_group = jax.random.randint(heavy_key, (), 0, GROUPS)
    weights = jax.random.randint(weight_key, (STORES, GROUPS), 1, 3)
    heavy_flag = jnp.arange(GROUPS)[None, :] == heavy_group
    weights = jnp.where(heavy_flag, 0, weights)
    remaining = VEC_DEV - SHARD_GROUP_SLOTS
    weight_total = jnp.sum(weights, axis=1, keepdims=True)
    even_row_share = remaining * weights // weight_total
    remainder_rows = remaining - jnp.sum(even_row_share, axis=1, keepdims=True)
    rank_positions = jnp.cumsum(jnp.where(heavy_flag, 0, 1), axis=1)
    extra_row_count = jnp.where(jnp.logical_and(jnp.logical_not(heavy_flag), rank_positions <= remainder_rows), 1, 0)
    return jnp.where(heavy_flag, SHARD_GROUP_SLOTS, even_row_share + extra_row_count).astype(jnp.int32)


def with_ends(array, own_key, smallest, top_value):
    longest = array.shape.index(max(array.shape))
    spots = []
    for shift in (0, 1):
        where = [jax.random.randint(jax.random.fold_in(own_key, axis), (), 0, length) for axis, length in enumerate(array.shape)]
        where[longest] = (where[longest] + shift) % array.shape[longest]
        spots.append(tuple(where))
    return array.at[spots[0]].set(smallest).at[spots[1]].set(top_value)


def shard_levels(key, extent, cuts, least, high):
    factor_of, own = 1.0, jax.random.fold_in(key, 6)
    for dim, blocks in cuts:
        heights = jnp.exp(jax.random.uniform(jax.random.fold_in(own, dim), (blocks,), jnp.float32, least / len(cuts), high / len(cuts)))
        factor_of = factor_of * jnp.repeat(heights, extent[dim] // blocks).reshape([-1 if axis == dim else 1 for axis in range(len(extent))])
    return factor_of


def rank_bounds(amount, skew):
    weights = [(1 << 20) // math.isqrt(grade ** skew) + 1 for grade in range(1, amount + 1)]
    scale = 1 + sum(weights) // (1 << 30)
    return np.cumsum(np.array([max(1, weight // scale) for weight in weights]))


def ranked(own_key, dims, number_of, slope):
    table = rank_bounds(number_of, slope)
    lot = jax.random.randint(jax.random.fold_in(own_key, 1), dims, 0, int(table[number_of - 1]))
    grade = jnp.searchsorted(jnp.asarray(table, jnp.int32), lot, side="right")
    return jax.random.permutation(jax.random.fold_in(own_key, 2), number_of)[grade].astype(jnp.int32)


def centred(own_key, extent, scale, limit, cuts=(), held_as=jnp.bfloat16):
    factor_of = shard_levels(own_key, extent, cuts, -0.22, 0.18) if cuts else 1.0
    values = jax.random.normal(own_key, extent, jnp.float32) * scale * factor_of
    return jnp.minimum(jnp.maximum(values, -limit), limit).astype(held_as)


def setup_inputs(seed: int = 0) -> dict:
    arg_keys = jax.random.split(jax.random.key(seed), 5)
    return {
        "vectors": centred(arg_keys[0], (ROWS, D), 1.0, 6.0, ((0, 32),)),
        "parents": with_ends(jax.random.randint(arg_keys[1], (ROWS,), 0, PAR_GRP), jax.random.fold_in(arg_keys[1], 1), 0, PAR_GRP - 1).astype(jnp.int32),
        "children": with_ends(ranked(arg_keys[2], (ROWS,), CHILD, 1), jax.random.fold_in(arg_keys[2], 3), 0, CHILD - 1).astype(jnp.int32),
        "counts": draw_counts(jax.random.fold_in(arg_keys[4], 71), 0),
    }


def pick_parent(all_dists, row_codes):
    row_count = all_dists.shape[0]
    stacked = all_dists.reshape(row_count, PAR_GRP, CHILD)
    parent_ids = jnp.maximum(row_codes, 0) // CHILD
    chosen = parent_ids[:, None, None] == jnp.arange(PAR_GRP, dtype=jnp.int32)[None, :, None]
    picked = jnp.sum(jnp.where(chosen, stacked, jnp.zeros((), jnp.float32)), axis=1)
    return jnp.where(row_codes[:, None] >= 0, picked, jnp.zeros((), jnp.float32))


def column_block(centroids, vec_norm, arrived):
    cent_wide = centroids.astype(jnp.float32)
    cent_norm = jnp.sum(cent_wide * cent_wide, axis=1)
    cross = jnp.dot(arrived, centroids.T, preferred_element_type=jnp.float32)
    return (vec_norm[:, None] - 2.0 * cross + cent_norm[None, :]) / D


def reference(vectors, parents, children, counts):
    shards = N_GRP * N_MEM
    width = PAR_GRP * CHILD
    stored = vectors.reshape(shards, VEC_DEV, D)
    parent_rows = parents.reshape(shards, VEC_DEV)
    child_rows = children.reshape(shards, VEC_DEV)
    offsets = (jnp.cumsum(counts, axis=1) - counts).astype(jnp.int32)
    slots = jnp.arange(SHARD_GROUP_SLOTS, dtype=jnp.int32)
    filled = slots[None, None, :] < counts[:, :, None]
    source_rows = jnp.where(filled, offsets[:, :, None] + slots[None, None, :], 0).astype(jnp.int32)
    flat_rows = source_rows.reshape(shards, N_GRP * SHARD_GROUP_SLOTS)
    flat_filled = filled.reshape(shards, N_GRP * SHARD_GROUP_SLOTS)
    sent = jnp.take_along_axis(stored, flat_rows[:, :, None], axis=1)
    sent = jnp.where(flat_filled[:, :, None], sent, jnp.zeros((), jnp.bfloat16))
    row_codes = jnp.take_along_axis(parent_rows, flat_rows, axis=1) * CHILD + jnp.take_along_axis(child_rows, flat_rows, axis=1)
    row_codes = jnp.where(flat_filled, row_codes, -1).astype(jnp.int32)
    sent = sent.reshape(N_GRP, N_MEM, N_GRP, SHARD_GROUP_SLOTS, D).transpose(2, 1, 0, 3, 4).reshape(N_GRP, N_MEM * N_GRP * SHARD_GROUP_SLOTS, D)
    row_codes = row_codes.reshape(N_GRP, N_MEM, N_GRP, SHARD_GROUP_SLOTS).transpose(2, 1, 0, 3).reshape(N_GRP, N_MEM * N_GRP * SHARD_GROUP_SLOTS)

    def one_group(paired):
        arrived, arrived_codes = paired
        segment_ids = jnp.where(arrived_codes >= 0, arrived_codes, width).astype(jnp.int32)
        vec_wide = arrived.astype(jnp.float32)
        child_sums = jax.ops.segment_sum(vec_wide, segment_ids, num_segments=width + 1)[:width]
        child_counts = jax.ops.segment_sum(jnp.ones(arrived_codes.shape, jnp.float32), segment_ids, num_segments=width + 1)[:width]
        centroids = (child_sums / jnp.maximum(child_counts, 1.0)[:, None]).astype(jnp.bfloat16)
        vec_norm = jnp.sum(vec_wide * vec_wide, axis=1)
        return pick_parent(column_block(centroids, vec_norm, arrived), arrived_codes)

    result = lax.map(one_group, (sent, row_codes))
    return result.reshape(N_GRP * N_MEM * N_GRP * SHARD_GROUP_SLOTS, CHILD)
```

```python
import functools

import jax
import jax.numpy as jnp
from jax import lax
from jax.experimental import pallas as pl
from jax.experimental.pallas import tpu as pltpu
from jax.sharding import PartitionSpec as P

CHILD = 1024
PAR_GRP = 2
WIDTH = PAR_GRP * CHILD
LOW = 32
MIB = 1024 * 1024


def inner_size(members):
    return max(d for d in range(1, members + 1) if members % d == 0 and d * d <= members)


def exchange_kernel(
    dims,
    counts_ref,
    vec_ref,
    par_ref,
    chi_ref,
    arr_out,
    cent_out,
    code_out,
    pick,
    out_codes,
    in_codes,
    group_codes,
    outgoing,
    arrived,
    member,
    sums,
    x_in,
    half,
    z_in,
    cent,
    sem_code,
    sem_vec,
    sem_xcode,
    sem_zcode,
    sem_x,
    sem_z,
    sem_zc,
    sem_xc,
    sem_local,
):
    groups, inner, outer, rows, cap, blocks, cols = dims
    slots = groups * cap
    share = WIDTH // inner
    part = share // outer
    g = lax.axis_index("grp")
    m = lax.axis_index("mem")
    zi, xi = m // inner, m % inner

    def grp_at(t):
        return (g + t) % groups

    def x_dev(t):
        return {"mem": zi * inner + (xi + t) % inner}

    def z_dev(t):
        return {"mem": ((zi + t) % outer) * inner + xi}

    barrier = pltpu.get_barrier_semaphore()
    for t in range(1, groups):
        pl.semaphore_signal(barrier, inc=1, device_id={"grp": grp_at(t)}, device_id_type=pl.DeviceIdType.MESH)
    for t in range(1, inner):
        pl.semaphore_signal(barrier, inc=1, device_id=x_dev(t), device_id_type=pl.DeviceIdType.MESH)
    for t in range(1, outer):
        pl.semaphore_signal(barrier, inc=1, device_id=z_dev(t), device_id_type=pl.DeviceIdType.MESH)

    def remote(src, dst, sems, where, device):
        return pltpu.make_async_remote_copy(
            src_ref=src,
            dst_ref=dst,
            send_sem=sems.at[(0,) + where],
            recv_sem=sems.at[(1,) + where],
            device_id=device,
            device_id_type=pl.DeviceIdType.MESH,
        )

    sent = []
    kept = []

    def send(*what):
        copy = remote(*what)
        copy.start()
        sent.append(copy)

    def keep(src, dst, number):
        copy = pltpu.make_async_copy(src, dst, sem_local.at[number])
        copy.start()
        kept.append(copy)

    code = par_ref[...] * CHILD + chi_ref[...]
    high = (code // LOW + 1).astype(jnp.float32)
    low = (code % LOW).astype(jnp.float32)
    first = lax.broadcasted_iota(jnp.int32, (16, rows), 0) == 0
    code_rows = jnp.where(first, high, low).astype(jnp.bfloat16)
    step = min(cap, 256)

    def make_pick(t):
        h = grp_at(t)
        count = counts_ref[0, h]
        offset = jnp.int32(0)
        for other in range(groups):
            offset = offset + jnp.where(other < h, counts_ref[0, other], 0)
        for base in range(0, cap, step):
            slot = lax.broadcasted_iota(jnp.int32, (step, rows), 0) + base
            row = lax.broadcasted_iota(jnp.int32, (step, rows), 1)
            chosen = jnp.logical_and(row - slot == offset, slot < count)
            pick[t, base : base + step, :] = jnp.where(chosen, 1.0, 0.0).astype(jnp.bfloat16)
        got = lax.dot_general(
            code_rows, pick[t], (((1,), (1,)), ((), ())), preferred_element_type=jnp.float32
        )
        value = (got[0:1] * LOW + got[1:2] - LOW).astype(jnp.int32)
        return jnp.broadcast_to(value, (8, cap))

    def picked(t, q):
        return jnp.dot(
            pick[t], vec_ref[:, q * cols : (q + 1) * cols], preferred_element_type=jnp.float32
        ).astype(jnp.bfloat16)

    def send_rows(t, q):
        outgoing[q, t - 1] = picked(t, q)
        send(outgoing.at[q, t - 1], arrived.at[q, g], sem_vec, (q, t - 1), {"grp": grp_at(t)})

    order = sorted(range(1, groups), key=lambda t: abs(2 * t - groups))
    for place, t in enumerate(order):
        out_codes[t - 1] = make_pick(t)
        outgoing[0, t - 1] = picked(t, 0)
        if place == 0:
            pl.semaphore_wait(barrier, groups + inner + outer - 3)
        send(out_codes.at[t - 1], in_codes.at[g], sem_code, (t - 1,), {"grp": grp_at(t)})
        send(outgoing.at[0, t - 1], arrived.at[0, g], sem_vec, (0, t - 1), {"grp": grp_at(t)})
    in_codes[g] = make_pick(0)
    arrived[0, g] = picked(0, 0)
    for q in range(1, blocks):
        for t in order:
            send_rows(t, q)
        arrived[q, g] = picked(0, q)

    for t in order:
        s = (g - t + groups) % groups
        remote(in_codes.at[s], in_codes.at[s], sem_code, (t - 1,), {"grp": grp_at(t)}).wait_recv()
    lanes = lax.broadcasted_iota(jnp.int32, group_codes.shape[2:], 0)
    mine = jnp.full(group_codes.shape[2:], -1, jnp.int32)
    for s in range(groups):
        mine = jnp.where(lanes == s, jnp.broadcast_to(in_codes[s, 0:1, :], mine.shape), mine)
    group_codes[0, 0] = mine
    for t in range(1, inner):
        send(group_codes.at[0, 0], group_codes.at[0, t], sem_xcode, (t - 1,), x_dev(t))
    keep(group_codes.at[0, 0], code_out, 0)

    tall = 256

    @pl.loop(0, WIDTH // tall)
    def _(i):
        ids = lax.broadcasted_iota(jnp.int32, (tall, cap), 0) + i * tall
        for s in range(groups):
            hit = ids == in_codes[s, 0:1, :]
            member[pl.ds(pl.multiple_of(i * tall, tall), tall), s * cap : (s + 1) * cap] = jnp.where(
                hit, 1.0, 0.0
            ).astype(jnp.bfloat16)

    def add_up(q):
        for t in order:
            s = (g - t + groups) % groups
            remote(
                arrived.at[q, s], arrived.at[q, s], sem_vec, (q, t - 1), {"grp": grp_at(t)}
            ).wait_recv()
        keep(arrived.at[q], arr_out.at[q], 1 + q)
        high_rows = min(share, 256)
        for t in [*range(1, inner), 0]:
            xt = (xi + t) % inner

            @pl.loop(0, share // high_rows)
            def _(i):
                start = pl.multiple_of(xt * share + i * high_rows, high_rows)
                total = jnp.dot(
                    member[pl.ds(start, high_rows), :],
                    arrived[q].reshape(slots, cols),
                    preferred_element_type=jnp.float32,
                )
                sums[q, xt, pl.ds(pl.multiple_of(i * high_rows, high_rows), high_rows), :] = total.astype(
                    jnp.bfloat16
                )

            if t:
                send(sums.at[q, xt], x_in.at[q, t - 1], sem_x, (q, t - 1), x_dev(t))

    def over_x(q):
        for t in range(1, inner):
            remote(x_in.at[q, t - 1], x_in.at[q, t - 1], sem_x, (q, t - 1), x_dev(t)).wait_recv()
        for t in [*range(1, outer), 0]:
            zt = (zi + t) % outer
            span = pl.ds(pl.multiple_of(zt * part, part), part)
            total = sums[q, xi, span, :].astype(jnp.float32)
            for u in range(inner - 1):
                total = total + x_in[q, u, span, :].astype(jnp.float32)
            half[q, zt] = total.astype(jnp.bfloat16)
            if t:
                send(half.at[q, zt], z_in.at[q, t - 1], sem_z, (q, t - 1), z_dev(t))

    def codes_over_x():
        for t in range(1, inner):
            remote(group_codes.at[0, t], group_codes.at[0, t], sem_xcode, (t - 1,), x_dev(t)).wait_recv()
        for t in range(1, outer):
            send(group_codes.at[0], group_codes.at[t], sem_zcode, (t - 1,), z_dev(t))

    def count_children():
        for t in range(1, outer):
            remote(group_codes.at[t], group_codes.at[t], sem_zcode, (t - 1,), z_dev(t)).wait_recv()
        ids = lax.broadcasted_iota(jnp.int32, (part, 128), 0) + (xi * outer + zi) * part

        def one_member(i, running):
            block = group_codes.at[i // inner, i % inner]
            for s in range(groups):
                for lane in range(0, cap, 128):
                    hit = ids == block[s : s + 1, lane : lane + 128]
                    running = running + jnp.where(hit, 1.0, 0.0)
            return running

        tally = lax.fori_loop(0, inner * outer, one_member, jnp.zeros((part, 128), jnp.float32))
        return jnp.maximum(jnp.sum(tally, axis=1, keepdims=True), 1.0)

    def over_z(q, tally):
        for t in range(1, outer):
            remote(z_in.at[q, t - 1], z_in.at[q, t - 1], sem_z, (q, t - 1), z_dev(t)).wait_recv()
        total = half[q, zi].astype(jnp.float32)
        for u in range(outer - 1):
            total = total + z_in[q, u].astype(jnp.float32)
        cent[q, xi, zi] = (total / tally).astype(jnp.bfloat16)
        for t in range(1, outer):
            send(cent.at[q, xi, zi], cent.at[q, xi, zi], sem_zc, (q, t - 1), z_dev(t))

    def back_over_z(q):
        for t in range(1, outer):
            zs = (zi - t + outer) % outer
            remote(cent.at[q, xi, zs], cent.at[q, xi, zs], sem_zc, (q, t - 1), z_dev(t)).wait_recv()
        for t in range(1, inner):
            send(cent.at[q, xi], cent.at[q, xi], sem_xc, (q, t - 1), x_dev(t))

    def back_over_x(q):
        for t in range(1, inner):
            xs = (xi - t + inner) % inner
            remote(cent.at[q, xs], cent.at[q, xs], sem_xc, (q, t - 1), x_dev(t)).wait_recv()
        keep(cent.at[q], cent_out.at[q], 1 + blocks + q)

    tally = None
    for beat in range(blocks + 4):
        if beat < blocks:
            add_up(beat)
        if beat == 0:
            codes_over_x()
        if 0 <= beat - 1 < blocks:
            over_x(beat - 1)
        if beat == 1:
            tally = count_children()
        if 0 <= beat - 2 < blocks:
            over_z(beat - 2, tally)
        if 0 <= beat - 3 < blocks:
            back_over_z(beat - 3)
        if 0 <= beat - 4 < blocks:
            back_over_x(beat - 4)

    for copy in kept:
        copy.wait()
    for copy in sent:
        copy.wait_send()


def distance_kernel(depth, arr_ref, cent_ref, code_ref, out_ref, norms):
    blocks = cent_ref.shape[0]

    @pl.when(pl.program_id(0) == 0)
    def _():
        for base in range(0, WIDTH, 128):
            square = jnp.zeros((128, 128), jnp.float32)
            for q in range(blocks):
                wide = cent_ref[q, base : base + 128, :].astype(jnp.float32)
                wide = wide * wide
                for lane in range(0, wide.shape[1], 128):
                    square = square + wide[:, lane : lane + 128]
            norms[:, base : base + 128] = jnp.broadcast_to(
                jnp.sum(square.T, axis=0, keepdims=True), (8, 128)
            )

    rows = arr_ref.shape[1]
    mark = pl.program_id(0)
    lanes = lax.broadcasted_iota(jnp.int32, code_ref.shape, 0)
    row_codes = jnp.sum(jnp.where(lanes == mark, code_ref[...], 0), axis=0, keepdims=True)
    column = jnp.broadcast_to(row_codes.astype(jnp.float32), (128, rows)).T[:, 0:1]
    x = jnp.concatenate([arr_ref[q] for q in range(blocks)], axis=1)
    wide = x.astype(jnp.float32)
    x_norm = jnp.sum(wide * wide, axis=1, keepdims=True)
    second = column >= CHILD
    filled = column >= 0
    step = 256
    for base in range(0, CHILD, step):
        values = []
        for p in range(PAR_GRP):
            start = p * CHILD + base
            c = jnp.concatenate([cent_ref[q, start : start + step, :] for q in range(blocks)], axis=1)
            cross = lax.dot_general(x, c, (((1,), (1,)), ((), ())), preferred_element_type=jnp.float32)
            values.append(norms[0:1, start : start + step] - 2.0 * cross)
        dist = (x_norm + jnp.where(second, values[1], values[0])) * (1.0 / depth)
        out_ref[:, base : base + step] = jnp.where(filled, dist, 0.0)


def body(vectors, parents, children, counts):
    groups = lax.axis_size("grp")
    members = lax.axis_size("mem")
    inner = inner_size(members)
    outer = members // inner
    rows, depth = vectors.shape
    cap = 2 * rows // groups
    slots = groups * cap
    cols = 256
    blocks = depth // cols
    share = WIDTH // inner
    part = share // outer
    code_high = max(8, groups)
    bf16, i32 = jnp.bfloat16, jnp.int32
    dims = (groups, inner, outer, rows, cap, blocks, cols)
    vmem = pltpu.VMEM
    dma = pltpu.SemaphoreType.DMA
    arr, cent, codes = pl.pallas_call(
        functools.partial(exchange_kernel, dims),
        out_shape=(
            jax.ShapeDtypeStruct((blocks, groups, cap, cols), bf16),
            jax.ShapeDtypeStruct((blocks, inner, outer, part, cols), bf16),
            jax.ShapeDtypeStruct((code_high, cap), i32),
        ),
        in_specs=[
            pl.BlockSpec(memory_space=pltpu.SMEM),
            pl.BlockSpec(memory_space=vmem),
            pl.BlockSpec(memory_space=vmem),
            pl.BlockSpec(memory_space=vmem),
        ],
        out_specs=(pl.BlockSpec(memory_space=pl.ANY),) * 3,
        scratch_shapes=[
            vmem((groups, cap, rows), bf16),
            vmem((groups - 1, 8, cap), i32),
            vmem((groups, 8, cap), i32),
            vmem((outer, inner, code_high, cap), i32),
            vmem((blocks, groups - 1, cap, cols), bf16),
            vmem((blocks, groups, cap, cols), bf16),
            vmem((WIDTH, slots), bf16),
            vmem((blocks, inner, share, cols), bf16),
            vmem((blocks, inner - 1, share, cols), bf16),
            vmem((blocks, outer, part, cols), bf16),
            vmem((blocks, outer - 1, part, cols), bf16),
            vmem((blocks, inner, outer, part, cols), bf16),
            dma((2, groups - 1)),
            dma((2, blocks, groups - 1)),
            dma((2, inner - 1)),
            dma((2, outer - 1)),
            dma((2, blocks, inner - 1)),
            dma((2, blocks, outer - 1)),
            dma((2, blocks, outer - 1)),
            dma((2, blocks, inner - 1)),
            dma((1 + 2 * blocks,)),
        ],
        compiler_params=pltpu.CompilerParams(
            collective_id=0, has_side_effects=True, vmem_limit_bytes=56 * MIB
        ),
    )(counts, vectors, parents.reshape(1, rows), children.reshape(1, rows))
    arr = arr.reshape(blocks, slots, cols)
    cent = cent.reshape(blocks, WIDTH, cols)
    return pl.pallas_call(
        functools.partial(distance_kernel, depth),
        grid=(groups,),
        out_shape=jax.ShapeDtypeStruct((slots, CHILD), jnp.float32),
        in_specs=[
            pl.BlockSpec((blocks, cap, cols), lambda i: (0, i, 0)),
            pl.BlockSpec((blocks, WIDTH, cols), lambda i: (0, 0, 0)),
            pl.BlockSpec((code_high, cap), lambda i: (0, 0)),
        ],
        out_specs=pl.BlockSpec((cap, CHILD), lambda i: (i, 0)),
        scratch_shapes=[vmem((8, WIDTH), jnp.float32)],
        compiler_params=pltpu.CompilerParams(vmem_limit_bytes=48 * MIB),
    )(arr, cent, codes)


def solution(mesh):
    in_specs = (
        P(("grp", "mem"), None),
        P(("grp", "mem")),
        P(("grp", "mem")),
        P(("grp", "mem"), None),
    )
    out_specs = P(("grp", "mem"), None)
    return jax.shard_map(body, mesh=mesh, in_specs=in_specs, out_specs=out_specs, check_vma=False)
```

```python
import functools

import jax
import jax.numpy as jnp
from jax import lax
from jax.experimental import pallas as pl
from jax.experimental.pallas import tpu as pltpu
from jax.sharding import PartitionSpec as P

CHILD = 1024
PAR_GRP = 2
WIDTH = PAR_GRP * CHILD
LOW = 32
MIB = 1024 * 1024
PIECES = 2


def inner_size(members):
    return max(d for d in range(1, members + 1) if members % d == 0 and d * d <= members)


def exchange_kernel(
    dims,
    counts_ref,
    vec_ref,
    par_ref,
    chi_ref,
    arr_out,
    cent_out,
    code_out,
    norm_out,
    pick,
    out_codes,
    in_codes,
    group_codes,
    outgoing,
    arrived,
    member,
    sums,
    x_in,
    half,
    z_in,
    cent,
    squares,
    norms,
    sem_code,
    sem_vec,
    sem_xcode,
    sem_zcode,
    sem_x,
    sem_z,
    sem_zc,
    sem_xc,
    sem_local,
):
    groups, inner, outer, rows, cap, blocks, cols = dims
    slots = groups * cap
    share = WIDTH // inner
    tall = share // PIECES
    part = tall // outer
    g = lax.axis_index("grp")
    m = lax.axis_index("mem")
    zi, xi = m // inner, m % inner

    def grp_at(t):
        return (g + t) % groups

    def x_dev(t):
        return {"mem": zi * inner + (xi + t) % inner}

    def z_dev(t):
        return {"mem": ((zi + t) % outer) * inner + xi}

    barrier = pltpu.get_barrier_semaphore()
    for t in range(1, groups):
        pl.semaphore_signal(barrier, inc=1, device_id={"grp": grp_at(t)}, device_id_type=pl.DeviceIdType.MESH)
    for t in range(1, inner):
        pl.semaphore_signal(barrier, inc=1, device_id=x_dev(t), device_id_type=pl.DeviceIdType.MESH)
    for t in range(1, outer):
        pl.semaphore_signal(barrier, inc=1, device_id=z_dev(t), device_id_type=pl.DeviceIdType.MESH)

    def remote(src, dst, sems, where, device):
        return pltpu.make_async_remote_copy(
            src_ref=src,
            dst_ref=dst,
            send_sem=sems.at[(0,) + where],
            recv_sem=sems.at[(1,) + where],
            device_id=device,
            device_id_type=pl.DeviceIdType.MESH,
        )

    sent = []
    kept = []

    def send(*what):
        copy = remote(*what)
        copy.start()
        sent.append(copy)

    def keep(src, dst, number):
        copy = pltpu.make_async_copy(src, dst, sem_local.at[number])
        copy.start()
        kept.append(copy)

    code = par_ref[...] * CHILD + chi_ref[...]
    high = (code // LOW + 1).astype(jnp.float32)
    low = (code % LOW).astype(jnp.float32)
    first = lax.broadcasted_iota(jnp.int32, (16, rows), 0) == 0
    code_rows = jnp.where(first, high, low).astype(jnp.bfloat16)
    step = min(cap, 256)

    def make_pick(t):
        h = grp_at(t)
        count = counts_ref[0, h]
        offset = jnp.int32(0)
        for other in range(groups):
            offset = offset + jnp.where(other < h, counts_ref[0, other], 0)
        for base in range(0, cap, step):
            slot = lax.broadcasted_iota(jnp.int32, (step, rows), 0) + base
            row = lax.broadcasted_iota(jnp.int32, (step, rows), 1)
            chosen = jnp.logical_and(row - slot == offset, slot < count)
            pick[t, base : base + step, :] = jnp.where(chosen, 1.0, 0.0).astype(jnp.bfloat16)
        got = lax.dot_general(
            code_rows, pick[t], (((1,), (1,)), ((), ())), preferred_element_type=jnp.float32
        )
        value = (got[0:1] * LOW + got[1:2] - LOW).astype(jnp.int32)
        return jnp.broadcast_to(value, (8, cap))

    def picked(t, q):
        return jnp.dot(
            pick[t], vec_ref[:, q * cols : (q + 1) * cols], preferred_element_type=jnp.float32
        ).astype(jnp.bfloat16)

    def send_rows(t, q):
        outgoing[q, t - 1] = picked(t, q)
        send(outgoing.at[q, t - 1], arrived.at[q, g], sem_vec, (q, t - 1), {"grp": grp_at(t)})

    order = sorted(range(1, groups), key=lambda t: abs(2 * t - groups))
    for place, t in enumerate(order):
        out_codes[t - 1] = make_pick(t)
        outgoing[0, t - 1] = picked(t, 0)
        if place == 0:
            pl.semaphore_wait(barrier, groups + inner + outer - 3)
        send(out_codes.at[t - 1], in_codes.at[g], sem_code, (t - 1,), {"grp": grp_at(t)})
        send(outgoing.at[0, t - 1], arrived.at[0, g], sem_vec, (0, t - 1), {"grp": grp_at(t)})
    in_codes[g] = make_pick(0)
    arrived[0, g] = picked(0, 0)
    for q in range(1, blocks):
        for t in order:
            send_rows(t, q)
        arrived[q, g] = picked(0, q)

    for t in order:
        s = (g - t + groups) % groups
        remote(in_codes.at[s], in_codes.at[s], sem_code, (t - 1,), {"grp": grp_at(t)}).wait_recv()
    lanes = lax.broadcasted_iota(jnp.int32, group_codes.shape[2:], 0)
    mine = jnp.full(group_codes.shape[2:], -1, jnp.int32)
    for s in range(groups):
        mine = jnp.where(lanes == s, jnp.broadcast_to(in_codes[s, 0:1, :], mine.shape), mine)
    group_codes[0, 0] = mine
    for t in range(1, inner):
        send(group_codes.at[0, 0], group_codes.at[0, t], sem_xcode, (t - 1,), x_dev(t))
    keep(group_codes.at[0, 0], code_out, 0)

    @pl.loop(0, WIDTH // 256)
    def _(i):
        ids = lax.broadcasted_iota(jnp.int32, (256, cap), 0) + i * 256
        for s in range(groups):
            hit = ids == in_codes[s, 0:1, :]
            member[pl.ds(pl.multiple_of(i * 256, 256), 256), s * cap : (s + 1) * cap] = jnp.where(
                hit, 1.0, 0.0
            ).astype(jnp.bfloat16)

    def add_up(q, r):
        if r == 0:
            for t in order:
                s = (g - t + groups) % groups
                remote(
                    arrived.at[q, s], arrived.at[q, s], sem_vec, (q, t - 1), {"grp": grp_at(t)}
                ).wait_recv()
            keep(arrived.at[q], arr_out.at[q], 2 + q)
        for t in [*range(1, inner), 0]:
            xt = (xi + t) % inner
            total = jnp.dot(
                member[pl.ds(pl.multiple_of(xt * share + r * tall, tall), tall), :],
                arrived[q].reshape(slots, cols),
                preferred_element_type=jnp.float32,
            )
            sums[q, r, xt] = total.astype(jnp.bfloat16)
            if t:
                send(sums.at[q, r, xt], x_in.at[q, r, t - 1], sem_x, (q, r, t - 1), x_dev(t))

    def over_x(q, r):
        for t in range(1, inner):
            remote(x_in.at[q, r, t - 1], x_in.at[q, r, t - 1], sem_x, (q, r, t - 1), x_dev(t)).wait_recv()
        for t in [*range(1, outer), 0]:
            zt = (zi + t) % outer
            span = pl.ds(pl.multiple_of(zt * part, part), part)
            total = sums[q, r, xi, span, :].astype(jnp.float32)
            for u in range(inner - 1):
                total = total + x_in[q, r, u, span, :].astype(jnp.float32)
            half[q, r, zt] = total.astype(jnp.bfloat16)
            if t:
                send(half.at[q, r, zt], z_in.at[q, r, t - 1], sem_z, (q, r, t - 1), z_dev(t))

    def codes_over_x():
        for t in range(1, inner):
            remote(group_codes.at[0, t], group_codes.at[0, t], sem_xcode, (t - 1,), x_dev(t)).wait_recv()
        for t in range(1, outer):
            send(group_codes.at[0], group_codes.at[t], sem_zcode, (t - 1,), z_dev(t))

    def codes_over_z():
        for t in range(1, outer):
            remote(group_codes.at[t], group_codes.at[t], sem_zcode, (t - 1,), z_dev(t)).wait_recv()

    def count_children(r):
        ids = lax.broadcasted_iota(jnp.int32, (part, 128), 0) + ((xi * PIECES + r) * outer + zi) * part

        def one_member(i, running):
            block = group_codes.at[i // inner, i % inner]
            for s in range(groups):
                for lane in range(0, cap, 128):
                    hit = ids == block[s : s + 1, lane : lane + 128]
                    running = running + jnp.where(hit, 1.0, 0.0)
            return running

        tally = lax.fori_loop(0, inner * outer, one_member, jnp.zeros((part, 128), jnp.float32))
        return jnp.maximum(jnp.sum(tally, axis=1, keepdims=True), 1.0)

    def over_z(q, r):
        for t in range(1, outer):
            remote(z_in.at[q, r, t - 1], z_in.at[q, r, t - 1], sem_z, (q, r, t - 1), z_dev(t)).wait_recv()
        total = half[q, r, zi].astype(jnp.float32)
        for u in range(outer - 1):
            total = total + z_in[q, r, u].astype(jnp.float32)
        cent[q, xi, r, zi] = (total / tallies[r]).astype(jnp.bfloat16)
        block = cent.at[q, xi, r, zi]
        for t in range(1, outer):
            send(block, block, sem_zc, (q, r, t - 1), z_dev(t))
        for t in range(1, inner):
            send(block, block, sem_xc, (q, r, 0, t - 1), x_dev(t))

    def back_over_z(q, r):
        for t in range(1, outer):
            block = cent.at[q, xi, r, (zi - t + outer) % outer]
            remote(block, block, sem_zc, (q, r, t - 1), z_dev(t)).wait_recv()
            for u in range(1, inner):
                send(block, block, sem_xc, (q, r, t, u - 1), x_dev(u))

    def back_over_x(q, r):
        for t in range(outer):
            for u in range(1, inner):
                block = cent.at[q, (xi - u + inner) % inner, r, (zi - t + outer) % outer]
                remote(block, block, sem_xc, (q, r, t, u - 1), x_dev(u)).wait_recv()
        for x in range(inner):
            keep(cent.at[q, x, r], cent_out.at[q, x, r], 2 + blocks + (q * PIECES + r) * inner + x)
        for x in range(inner):
            for base in range(0, tall, 128):
                wide = cent[q, x, r].reshape(tall, cols)[base : base + 128].astype(jnp.float32)
                wide = wide * wide
                square = wide[:, 0:128]
                for lane in range(128, cols, 128):
                    square = square + wide[:, lane : lane + 128]
                child = (x * PIECES + r) * tall + base
                if q > 0:
                    square = square + squares[child : child + 128, :]
                if q < blocks - 1:
                    squares[child : child + 128, :] = square
                else:
                    norms[:, child : child + 128] = jnp.broadcast_to(
                        jnp.sum(square.T, axis=0, keepdims=True), (8, 128)
                    )

    tasks = []
    for q in range(blocks):
        for r in range(PIECES):
            sum_at = 22.0 * q + r
            x_at = 22.0 * q + 12.0 + 11.0 * r
            stages = (add_up, over_x, over_z, back_over_z, back_over_x)
            for number, stage in enumerate(stages):
                when = sum_at if number == 0 else x_at + 12.0 * (number - 1)
                tasks.append((when / 2.0, number, stage, (q, r)))
    tasks.append((1.5, 9, codes_over_x, ()))
    tasks.append((8.5, 9, codes_over_z, ()))
    tallies = []
    for r in range(PIECES):
        tasks.append((8.6 + r / 10, 9, lambda number: tallies.append(count_children(number)), (r,)))
    for when, number, stage, where in sorted(tasks, key=lambda task: task[:2]):
        stage(*where)

    keep(norms, norm_out, 1)
    for copy in kept:
        copy.wait()
    for copy in sent:
        copy.wait_send()


def distance_kernel(depth, arr_ref, cent_ref, code_ref, norm_ref, out_ref):
    blocks, rows = arr_ref.shape[:2]
    mark = pl.program_id(0)
    lanes = lax.broadcasted_iota(jnp.int32, code_ref.shape, 0)
    row_codes = jnp.sum(jnp.where(lanes == mark, code_ref[...], 0), axis=0, keepdims=True)
    column = jnp.broadcast_to(row_codes.astype(jnp.float32), (128, rows)).T[:, 0:1]
    x = jnp.concatenate([arr_ref[q] for q in range(blocks)], axis=1)
    wide = x.astype(jnp.float32)
    second = column >= CHILD
    filled = column >= 0
    x_norm = jnp.sum(wide * wide, axis=1, keepdims=True) * (1.0 / depth)
    step = 256
    for base in range(0, CHILD, step):
        crosses, squares = [], []
        for p in range(PAR_GRP):
            start = p * CHILD + base
            c = jnp.concatenate([cent_ref[q, start : start + step, :] for q in range(blocks)], axis=1)
            crosses.append(
                lax.dot_general(x, c, (((1,), (1,)), ((), ())), preferred_element_type=jnp.float32)
            )
            squares.append(norm_ref[0:1, start : start + step] * (1.0 / depth))
        cross = jnp.where(second, crosses[1], crosses[0])
        square = jnp.where(second, squares[1], squares[0])
        dist = (x_norm + square) - cross * (2.0 / depth)
        out_ref[:, base : base + step] = jnp.where(filled, dist, 0.0)


def body(vectors, parents, children, counts):
    groups = lax.axis_size("grp")
    members = lax.axis_size("mem")
    inner = inner_size(members)
    outer = members // inner
    rows, depth = vectors.shape
    cap = 2 * rows // groups
    slots = groups * cap
    cols = 256
    blocks = depth // cols
    share = WIDTH // inner
    tall = share // PIECES
    part = tall // outer
    code_high = max(8, groups)
    bf16, i32 = jnp.bfloat16, jnp.int32
    dims = (groups, inner, outer, rows, cap, blocks, cols)
    vmem = pltpu.VMEM
    dma = pltpu.SemaphoreType.DMA
    arr, cent, codes, norms = pl.pallas_call(
        functools.partial(exchange_kernel, dims),
        out_shape=(
            jax.ShapeDtypeStruct((blocks, groups, cap, cols), bf16),
            jax.ShapeDtypeStruct((blocks, inner, PIECES, outer, part, cols), bf16),
            jax.ShapeDtypeStruct((code_high, cap), i32),
            jax.ShapeDtypeStruct((8, WIDTH), jnp.float32),
        ),
        in_specs=[
            pl.BlockSpec(memory_space=pltpu.SMEM),
            pl.BlockSpec(memory_space=vmem),
            pl.BlockSpec(memory_space=vmem),
            pl.BlockSpec(memory_space=vmem),
        ],
        out_specs=(pl.BlockSpec(memory_space=pl.ANY),) * 4,
        scratch_shapes=[
            vmem((groups, cap, rows), bf16),
            vmem((groups - 1, 8, cap), i32),
            vmem((groups, 8, cap), i32),
            vmem((outer, inner, code_high, cap), i32),
            vmem((blocks, groups - 1, cap, cols), bf16),
            vmem((blocks, groups, cap, cols), bf16),
            vmem((WIDTH, slots), bf16),
            vmem((blocks, PIECES, inner, tall, cols), bf16),
            vmem((blocks, PIECES, inner - 1, tall, cols), bf16),
            vmem((blocks, PIECES, outer, part, cols), bf16),
            vmem((blocks, PIECES, outer - 1, part, cols), bf16),
            vmem((blocks, inner, PIECES, outer, part, cols), bf16),
            vmem((WIDTH, 128), jnp.float32),
            vmem((8, WIDTH), jnp.float32),
            dma((2, groups - 1)),
            dma((2, blocks, groups - 1)),
            dma((2, inner - 1)),
            dma((2, outer - 1)),
            dma((2, blocks, PIECES, inner - 1)),
            dma((2, blocks, PIECES, outer - 1)),
            dma((2, blocks, PIECES, outer - 1)),
            dma((2, blocks, PIECES, outer, inner - 1)),
            dma((2 + blocks + blocks * PIECES * inner,)),
        ],
        compiler_params=pltpu.CompilerParams(
            collective_id=0, has_side_effects=True, vmem_limit_bytes=56 * MIB
        ),
    )(counts, vectors, parents.reshape(1, rows), children.reshape(1, rows))
    arr = arr.reshape(blocks, slots, cols)
    cent = cent.reshape(blocks, WIDTH, cols)
    return pl.pallas_call(
        functools.partial(distance_kernel, depth),
        grid=(groups,),
        out_shape=jax.ShapeDtypeStruct((slots, CHILD), jnp.float32),
        in_specs=[
            pl.BlockSpec((blocks, cap, cols), lambda i: (0, i, 0)),
            pl.BlockSpec((blocks, WIDTH, cols), lambda i: (0, 0, 0)),
            pl.BlockSpec((code_high, cap), lambda i: (0, 0)),
            pl.BlockSpec((8, WIDTH), lambda i: (0, 0)),
        ],
        out_specs=pl.BlockSpec((cap, CHILD), lambda i: (i, 0)),
        compiler_params=pltpu.CompilerParams(vmem_limit_bytes=60 * MIB),
    )(arr, cent, codes, norms)


def solution(mesh):
    in_specs = (
        P(("grp", "mem"), None),
        P(("grp", "mem")),
        P(("grp", "mem")),
        P(("grp", "mem"), None),
    )
    out_specs = P(("grp", "mem"), None)
    return jax.shard_map(body, mesh=mesh, in_specs=in_specs, out_specs=out_specs, check_vma=False)
```

```python
import functools

import jax
import jax.numpy as jnp
from jax import lax
from jax.experimental import pallas as pl
from jax.experimental.pallas import tpu as pltpu
from jax.sharding import PartitionSpec as P

CHILD = 1024
PAR_GRP = 2
WIDTH = PAR_GRP * CHILD
LOW = 32
MIB = 1024 * 1024
PIECES = 1


def inner_size(members):
    return max(d for d in range(1, members + 1) if members % d == 0 and d * d <= members)


def exchange_kernel(
    dims,
    counts_ref,
    vec_ref,
    par_ref,
    chi_ref,
    arr_out,
    cent_out,
    code_out,
    norm_out,
    pick,
    out_codes,
    in_codes,
    group_codes,
    outgoing,
    arrived,
    member,
    sums,
    x_in,
    half,
    z_in,
    cent,
    squares,
    norms,
    sem_code,
    sem_vec,
    sem_xcode,
    sem_zcode,
    sem_x,
    sem_z,
    sem_zc,
    sem_xc,
    sem_local,
):
    groups, inner, outer, rows, cap, blocks, cols = dims
    slots = groups * cap
    share = WIDTH // inner
    tall = share // PIECES
    part = tall // outer
    g = lax.axis_index("grp")
    m = lax.axis_index("mem")
    zi, xi = m // inner, m % inner

    def grp_at(t):
        return (g + t) % groups

    def x_dev(t):
        return {"mem": zi * inner + (xi + t) % inner}

    def z_dev(t):
        return {"mem": ((zi + t) % outer) * inner + xi}

    barrier = pltpu.get_barrier_semaphore()
    for t in range(1, groups):
        pl.semaphore_signal(barrier, inc=1, device_id={"grp": grp_at(t)}, device_id_type=pl.DeviceIdType.MESH)
    for t in range(1, inner):
        pl.semaphore_signal(barrier, inc=1, device_id=x_dev(t), device_id_type=pl.DeviceIdType.MESH)
    for t in range(1, outer):
        pl.semaphore_signal(barrier, inc=1, device_id=z_dev(t), device_id_type=pl.DeviceIdType.MESH)

    def remote(src, dst, sems, where, device):
        return pltpu.make_async_remote_copy(
            src_ref=src,
            dst_ref=dst,
            send_sem=sems.at[(0,) + where],
            recv_sem=sems.at[(1,) + where],
            device_id=device,
            device_id_type=pl.DeviceIdType.MESH,
        )

    sent = []
    kept = []

    def send(*what):
        copy = remote(*what)
        copy.start()
        sent.append(copy)

    def keep(src, dst, number):
        copy = pltpu.make_async_copy(src, dst, sem_local.at[number])
        copy.start()
        kept.append(copy)

    code = par_ref[...] * CHILD + chi_ref[...]
    high = (code // LOW + 1).astype(jnp.float32)
    low = (code % LOW).astype(jnp.float32)
    first = lax.broadcasted_iota(jnp.int32, (16, rows), 0) == 0
    code_rows = jnp.where(first, high, low).astype(jnp.bfloat16)
    step = min(cap, 256)

    def make_pick(t):
        h = grp_at(t)
        count = counts_ref[0, h]
        offset = jnp.int32(0)
        for other in range(groups):
            offset = offset + jnp.where(other < h, counts_ref[0, other], 0)
        for base in range(0, cap, step):
            slot = lax.broadcasted_iota(jnp.int32, (step, rows), 0) + base
            row = lax.broadcasted_iota(jnp.int32, (step, rows), 1)
            chosen = jnp.logical_and(row - slot == offset, slot < count)
            pick[t, base : base + step, :] = jnp.where(chosen, 1.0, 0.0).astype(jnp.bfloat16)
        got = lax.dot_general(
            code_rows, pick[t], (((1,), (1,)), ((), ())), preferred_element_type=jnp.float32
        )
        value = (got[0:1] * LOW + got[1:2] - LOW).astype(jnp.int32)
        return jnp.broadcast_to(value, (8, cap))

    batches = [(0,), (1,)] + [tuple(range(q, min(q + 2, blocks))) for q in range(2, blocks, 2)]

    def pick_rows(t, batch):
        rows_of = vec_ref[:, batch[0] * cols : (batch[-1] + 1) * cols]
        found = jnp.dot(pick[t], rows_of, preferred_element_type=jnp.float32).astype(jnp.bfloat16)
        for place, q in enumerate(batch):
            block = found[:, place * cols : (place + 1) * cols]
            if t:
                outgoing[q, t - 1] = block
            else:
                arrived[q, g] = block

    def send_rows(t, batch):
        for q in batch:
            send(outgoing.at[q, t - 1], arrived.at[q, g], sem_vec, (q, t - 1), {"grp": grp_at(t)})

    order = sorted(range(1, groups), key=lambda t: abs(2 * t - groups))
    for place, t in enumerate(order):
        out_codes[t - 1] = make_pick(t)
        pick_rows(t, batches[0])
        if place == 0:
            pl.semaphore_wait(barrier, groups + inner + outer - 3)
        send(out_codes.at[t - 1], in_codes.at[g], sem_code, (t - 1,), {"grp": grp_at(t)})
        send_rows(t, batches[0])
    for t in order:
        pick_rows(t, batches[1])
        send_rows(t, batches[1])
    in_codes[g] = make_pick(0)
    pick_rows(0, batches[0])

    def pick_later():
        for batch in batches[2:]:
            for t in order:
                pick_rows(t, batch)
                send_rows(t, batch)
        for batch in batches[1:]:
            pick_rows(0, batch)

    for t in order:
        s = (g - t + groups) % groups
        remote(in_codes.at[s], in_codes.at[s], sem_code, (t - 1,), {"grp": grp_at(t)}).wait_recv()
    lanes = lax.broadcasted_iota(jnp.int32, group_codes.shape[2:], 0)
    mine = jnp.full(group_codes.shape[2:], -1, jnp.int32)
    for s in range(groups):
        mine = jnp.where(lanes == s, jnp.broadcast_to(in_codes[s, 0:1, :], mine.shape), mine)
    group_codes[0, 0] = mine
    for t in range(1, inner):
        send(group_codes.at[0, 0], group_codes.at[0, t], sem_xcode, (t - 1,), x_dev(t))
    keep(group_codes.at[0, 0], code_out, 0)

    @pl.loop(0, WIDTH // 256)
    def _(i):
        ids = lax.broadcasted_iota(jnp.int32, (256, cap), 0) + i * 256
        for s in range(groups):
            hit = ids == in_codes[s, 0:1, :]
            member[pl.ds(pl.multiple_of(i * 256, 256), 256), s * cap : (s + 1) * cap] = jnp.where(
                hit, 1.0, 0.0
            ).astype(jnp.bfloat16)

    def add_up(*batch):
        for q in batch:
            for t in order:
                s = (g - t + groups) % groups
                remote(
                    arrived.at[q, s], arrived.at[q, s], sem_vec, (q, t - 1), {"grp": grp_at(t)}
                ).wait_recv()
            keep(arrived.at[q], arr_out.at[q], 2 + q)
        rows_of = jnp.concatenate([arrived[q].reshape(slots, cols) for q in batch], axis=1)
        for t in [*range(1, inner), 0]:
            xt = (xi + t) % inner
            for r in range(PIECES):
                total = jnp.dot(
                    member[pl.ds(pl.multiple_of(xt * share + r * tall, tall), tall), :],
                    rows_of,
                    preferred_element_type=jnp.float32,
                ).astype(jnp.bfloat16)
                for place, q in enumerate(batch):
                    sums[q, r, xt] = total[:, place * cols : (place + 1) * cols]
                    if t:
                        send(sums.at[q, r, xt], x_in.at[q, r, t - 1], sem_x, (q, r, t - 1), x_dev(t))

    def over_x(q, r):
        for t in range(1, inner):
            remote(x_in.at[q, r, t - 1], x_in.at[q, r, t - 1], sem_x, (q, r, t - 1), x_dev(t)).wait_recv()
        for t in [*range(1, outer), 0]:
            zt = (zi + t) % outer
            span = pl.ds(pl.multiple_of(zt * part, part), part)
            total = sums[q, r, xi, span, :].astype(jnp.float32)
            for u in range(inner - 1):
                total = total + x_in[q, r, u, span, :].astype(jnp.float32)
            half[q, r, zt] = total.astype(jnp.bfloat16)
            if t:
                send(half.at[q, r, zt], z_in.at[q, r, t - 1], sem_z, (q, r, t - 1), z_dev(t))

    def codes_over_x():
        for t in range(1, inner):
            remote(group_codes.at[0, t], group_codes.at[0, t], sem_xcode, (t - 1,), x_dev(t)).wait_recv()
        for t in range(1, outer):
            send(group_codes.at[0], group_codes.at[t], sem_zcode, (t - 1,), z_dev(t))

    def codes_over_z():
        for t in range(1, outer):
            remote(group_codes.at[t], group_codes.at[t], sem_zcode, (t - 1,), z_dev(t)).wait_recv()

    def count_children(r):
        ids = lax.broadcasted_iota(jnp.int32, (part, 128), 0) + ((xi * PIECES + r) * outer + zi) * part

        def one_member(i, running):
            block = group_codes.at[i // inner, i % inner]
            for s in range(groups):
                for lane in range(0, cap, 128):
                    hit = ids == block[s : s + 1, lane : lane + 128]
                    running = running + jnp.where(hit, 1.0, 0.0)
            return running

        tally = lax.fori_loop(0, inner * outer, one_member, jnp.zeros((part, 128), jnp.float32))
        return jnp.maximum(jnp.sum(tally, axis=1, keepdims=True), 1.0)

    def over_z(q, r):
        for t in range(1, outer):
            remote(z_in.at[q, r, t - 1], z_in.at[q, r, t - 1], sem_z, (q, r, t - 1), z_dev(t)).wait_recv()
        total = half[q, r, zi].astype(jnp.float32)
        for u in range(outer - 1):
            total = total + z_in[q, r, u].astype(jnp.float32)
        cent[q, xi, r, zi] = (total / tallies[r]).astype(jnp.bfloat16)
        block = cent.at[q, xi, r, zi]
        for t in range(1, outer):
            send(block, block, sem_zc, (q, r, t - 1), z_dev(t))
        for t in range(1, inner):
            send(block, block, sem_xc, (q, r, 0, t - 1), x_dev(t))

    def add_squares(q, x, r):
        for base in range(0, tall, 128):
            wide = cent[q, x, r].reshape(tall, cols)[base : base + 128].astype(jnp.float32)
            square = wide * wide
            child = pl.ds(pl.multiple_of((x * PIECES + r) * tall + base, 128), 128)
            if q > 0:
                square = square + squares[child, :]
            if q < blocks - 1:
                squares[child, :] = square
            else:
                norms[:, child] = jnp.broadcast_to(jnp.sum(square.T, axis=0, keepdims=True), (8, 128))

    def write_cent(q, x, r, number):
        keep(cent.at[q, x, r], cent_out.at[q, x, r], 2 + blocks + (q * PIECES + r) * inner + number)

    def back_over_z(q, r):
        for t in range(1, outer):
            block = cent.at[q, xi, r, (zi - t + outer) % outer]
            remote(block, block, sem_zc, (q, r, t - 1), z_dev(t)).wait_recv()
            for u in range(1, inner):
                send(block, block, sem_xc, (q, r, t, u - 1), x_dev(u))
        write_cent(q, xi, r, 0)
        add_squares(q, xi, r)

    def back_over_x(q, r):
        for u in range(1, inner):
            x = (xi - u + inner) % inner
            for t in range(outer):
                block = cent.at[q, x, r, (zi - t + outer) % outer]
                remote(block, block, sem_xc, (q, r, t, u - 1), x_dev(u)).wait_recv()
            write_cent(q, x, r, u)
            add_squares(q, x, r)

    tasks = []
    free = 0.0
    for number, batch in enumerate(batches):
        ready = 7.0 * batch[-1]
        tasks.append((ready, 0, add_up, batch))
        for q in batch:
            free = max(free, ready + 1.0) + 7.0
            for r in range(PIECES):
                for number, stage in enumerate((over_x, over_z, back_over_z, back_over_x)):
                    tasks.append((free + 7.0 * number, number + 1, stage, (q, r)))
    tasks.append((0.5, 8, codes_over_x, ()))
    tasks.append((9.2, 8, codes_over_z, ()))
    tallies = []
    for r in range(PIECES):
        tasks.append((9.3, 9, lambda number: tallies.append(count_children(number)), (r,)))
    pick_later()
    for when, number, stage, where in sorted(tasks, key=lambda task: task[:2]):
        stage(*where)

    keep(norms, norm_out, 1)
    for copy in kept:
        copy.wait()
    for copy in sent:
        copy.wait_send()


def distance_kernel(depth, arr_ref, cent_ref, code_ref, norm_ref, out_ref):
    blocks, rows = arr_ref.shape[:2]
    mark = pl.program_id(0)
    lanes = lax.broadcasted_iota(jnp.int32, code_ref.shape, 0)
    row_codes = jnp.sum(jnp.where(lanes == mark, code_ref[...], 0), axis=0, keepdims=True)
    column = jnp.broadcast_to(row_codes.astype(jnp.float32), (128, rows)).T[:, 0:1]
    x = jnp.concatenate([arr_ref[q] for q in range(blocks)], axis=1)
    wide = x.astype(jnp.float32)
    second = column >= CHILD
    filled = column >= 0
    x_norm = jnp.sum(wide * wide, axis=1, keepdims=True) * (1.0 / depth)
    step = 256
    for base in range(0, CHILD, step):
        crosses, squares = [], []
        for p in range(PAR_GRP):
            start = p * CHILD + base
            c = jnp.concatenate([cent_ref[q, start : start + step, :] for q in range(blocks)], axis=1)
            crosses.append(
                lax.dot_general(x, c, (((1,), (1,)), ((), ())), preferred_element_type=jnp.float32)
            )
            squares.append(norm_ref[0:1, start : start + step] * (1.0 / depth))
        cross = jnp.where(second, crosses[1], crosses[0])
        square = jnp.where(second, squares[1], squares[0])
        dist = (x_norm + square) - cross * (2.0 / depth)
        out_ref[:, base : base + step] = jnp.where(filled, dist, 0.0)


def body(vectors, parents, children, counts):
    groups = lax.axis_size("grp")
    members = lax.axis_size("mem")
    inner = inner_size(members)
    outer = members // inner
    rows, depth = vectors.shape
    cap = 2 * rows // groups
    slots = groups * cap
    cols = 128
    blocks = depth // cols
    share = WIDTH // inner
    tall = share // PIECES
    part = tall // outer
    code_high = max(8, groups)
    bf16, i32 = jnp.bfloat16, jnp.int32
    dims = (groups, inner, outer, rows, cap, blocks, cols)
    vmem = pltpu.VMEM
    dma = pltpu.SemaphoreType.DMA
    arr, cent, codes, norms = pl.pallas_call(
        functools.partial(exchange_kernel, dims),
        out_shape=(
            jax.ShapeDtypeStruct((blocks, groups, cap, cols), bf16),
            jax.ShapeDtypeStruct((blocks, inner, PIECES, outer, part, cols), bf16),
            jax.ShapeDtypeStruct((code_high, cap), i32),
            jax.ShapeDtypeStruct((8, WIDTH), jnp.float32),
        ),
        in_specs=[
            pl.BlockSpec(memory_space=pltpu.SMEM),
            pl.BlockSpec(memory_space=vmem),
            pl.BlockSpec(memory_space=vmem),
            pl.BlockSpec(memory_space=vmem),
        ],
        out_specs=(pl.BlockSpec(memory_space=pl.ANY),) * 4,
        scratch_shapes=[
            vmem((groups, cap, rows), bf16),
            vmem((groups - 1, 8, cap), i32),
            vmem((groups, 8, cap), i32),
            vmem((outer, inner, code_high, cap), i32),
            vmem((blocks, groups - 1, cap, cols), bf16),
            vmem((blocks, groups, cap, cols), bf16),
            vmem((WIDTH, slots), bf16),
            vmem((blocks, PIECES, inner, tall, cols), bf16),
            vmem((blocks, PIECES, inner - 1, tall, cols), bf16),
            vmem((blocks, PIECES, outer, part, cols), bf16),
            vmem((blocks, PIECES, outer - 1, part, cols), bf16),
            vmem((blocks, inner, PIECES, outer, part, cols), bf16),
            vmem((WIDTH, 128), jnp.float32),
            vmem((8, WIDTH), jnp.float32),
            dma((2, groups - 1)),
            dma((2, blocks, groups - 1)),
            dma((2, inner - 1)),
            dma((2, outer - 1)),
            dma((2, blocks, PIECES, inner - 1)),
            dma((2, blocks, PIECES, outer - 1)),
            dma((2, blocks, PIECES, outer - 1)),
            dma((2, blocks, PIECES, outer, inner - 1)),
            dma((2 + blocks + blocks * PIECES * inner,)),
        ],
        compiler_params=pltpu.CompilerParams(
            collective_id=0, has_side_effects=True, vmem_limit_bytes=56 * MIB
        ),
    )(counts, vectors, parents.reshape(1, rows), children.reshape(1, rows))
    arr = arr.reshape(blocks, slots, cols)
    cent = cent.reshape(blocks, WIDTH, cols)
    return pl.pallas_call(
        functools.partial(distance_kernel, depth),
        grid=(groups,),
        out_shape=jax.ShapeDtypeStruct((slots, CHILD), jnp.float32),
        in_specs=[
            pl.BlockSpec((blocks, cap, cols), lambda i: (0, i, 0)),
            pl.BlockSpec((blocks, WIDTH, cols), lambda i: (0, 0, 0)),
            pl.BlockSpec((code_high, cap), lambda i: (0, 0)),
            pl.BlockSpec((8, WIDTH), lambda i: (0, 0)),
        ],
        out_specs=pl.BlockSpec((cap, CHILD), lambda i: (i, 0)),
        compiler_params=pltpu.CompilerParams(vmem_limit_bytes=60 * MIB),
    )(arr, cent, codes, norms)


def solution(mesh):
    in_specs = (
        P(("grp", "mem"), None),
        P(("grp", "mem")),
        P(("grp", "mem")),
        P(("grp", "mem"), None),
    )
    out_specs = P(("grp", "mem"), None)
    return jax.shard_map(body, mesh=mesh, in_specs=in_specs, out_specs=out_specs, check_vma=False)
```

```python
import functools

import jax
import jax.numpy as jnp
from jax import lax
from jax.experimental import pallas as pl
from jax.experimental.pallas import tpu as pltpu
from jax.sharding import PartitionSpec as P

CHILD = 1024
PAR_GRP = 2
WIDTH = PAR_GRP * CHILD
LOW = 32
MIB = 1024 * 1024
PIECES = 2


def inner_size(members):
    return max(d for d in range(1, members + 1) if members % d == 0 and d * d <= members)


def exchange_kernel(
    dims,
    counts_ref,
    vec_ref,
    par_ref,
    chi_ref,
    arr_out,
    cent_out,
    code_out,
    norm_out,
    pick,
    out_codes,
    in_codes,
    group_codes,
    outgoing,
    arrived,
    member,
    sums,
    x_in,
    half,
    z_near,
    pair,
    z_far,
    cent,
    squares,
    norms,
    sem_code,
    sem_vec,
    sem_xcode,
    sem_zcode,
    sem_x,
    sem_z,
    sem_zc,
    sem_xc,
    sem_local,
):
    groups, inner, outer, rows, cap, blocks, cols = dims
    slots = groups * cap
    share = WIDTH // inner
    tall = share // PIECES
    part = tall // outer
    g = lax.axis_index("grp")
    m = lax.axis_index("mem")
    zi, xi = m // inner, m % inner
    duos = outer // 2
    side, duo = zi % 2, zi // 2
    next_z = zi + 1 - 2 * side

    def far_z(t):
        return 2 * ((duo + t) % duos) + side

    def grp_at(t):
        return (g + t) % groups

    def x_dev(t):
        return {"mem": zi * inner + (xi + t) % inner}

    def z_dev(t):
        return {"mem": ((zi + t) % outer) * inner + xi}

    def at_z(z):
        return {"mem": z * inner + xi}

    barrier = pltpu.get_barrier_semaphore()
    for t in range(1, groups):
        pl.semaphore_signal(barrier, inc=1, device_id={"grp": grp_at(t)}, device_id_type=pl.DeviceIdType.MESH)
    for t in range(1, inner):
        pl.semaphore_signal(barrier, inc=1, device_id=x_dev(t), device_id_type=pl.DeviceIdType.MESH)
    for t in range(1, outer):
        pl.semaphore_signal(barrier, inc=1, device_id=z_dev(t), device_id_type=pl.DeviceIdType.MESH)

    def remote(src, dst, sems, where, device):
        return pltpu.make_async_remote_copy(
            src_ref=src,
            dst_ref=dst,
            send_sem=sems.at[(0,) + where],
            recv_sem=sems.at[(1,) + where],
            device_id=device,
            device_id_type=pl.DeviceIdType.MESH,
        )

    sent = []
    kept = []

    def send(*what):
        copy = remote(*what)
        copy.start()
        sent.append(copy)

    def keep(src, dst, number):
        copy = pltpu.make_async_copy(src, dst, sem_local.at[number])
        copy.start()
        kept.append(copy)

    code = par_ref[...] * CHILD + chi_ref[...]
    high = (code // LOW + 1).astype(jnp.float32)
    low = (code % LOW).astype(jnp.float32)
    first = lax.broadcasted_iota(jnp.int32, (16, rows), 0) == 0
    code_rows = jnp.where(first, high, low).astype(jnp.bfloat16)
    step = min(cap, 256)

    def make_pick(t):
        h = grp_at(t)
        count = counts_ref[0, h]
        offset = jnp.int32(0)
        for other in range(groups):
            offset = offset + jnp.where(other < h, counts_ref[0, other], 0)
        for base in range(0, cap, step):
            slot = lax.broadcasted_iota(jnp.int32, (step, rows), 0) + base
            row = lax.broadcasted_iota(jnp.int32, (step, rows), 1)
            chosen = jnp.logical_and(row - slot == offset, slot < count)
            pick[t, base : base + step, :] = jnp.where(chosen, 1.0, 0.0).astype(jnp.bfloat16)
        got = lax.dot_general(
            code_rows, pick[t], (((1,), (1,)), ((), ())), preferred_element_type=jnp.float32
        )
        value = (got[0:1] * LOW + got[1:2] - LOW).astype(jnp.int32)
        return jnp.broadcast_to(value, (8, cap))

    def picked(t, q):
        return jnp.dot(
            pick[t], vec_ref[:, q * cols : (q + 1) * cols], preferred_element_type=jnp.float32
        ).astype(jnp.bfloat16)

    def send_rows(t, q):
        outgoing[q, t - 1] = picked(t, q)
        send(outgoing.at[q, t - 1], arrived.at[q, g], sem_vec, (q, t - 1), {"grp": grp_at(t)})

    order = sorted(range(1, groups), key=lambda t: abs(2 * t - groups))
    for place, t in enumerate(order):
        out_codes[t - 1] = make_pick(t)
        outgoing[0, t - 1] = picked(t, 0)
        if place == 0:
            pl.semaphore_wait(barrier, groups + inner + outer - 3)
        send(out_codes.at[t - 1], in_codes.at[g], sem_code, (t - 1,), {"grp": grp_at(t)})
        send(outgoing.at[0, t - 1], arrived.at[0, g], sem_vec, (0, t - 1), {"grp": grp_at(t)})
    in_codes[g] = make_pick(0)
    arrived[0, g] = picked(0, 0)
    for q in range(1, blocks):
        for t in order:
            send_rows(t, q)
        arrived[q, g] = picked(0, q)

    for t in order:
        s = (g - t + groups) % groups
        remote(in_codes.at[s], in_codes.at[s], sem_code, (t - 1,), {"grp": grp_at(t)}).wait_recv()
    lanes = lax.broadcasted_iota(jnp.int32, group_codes.shape[2:], 0)
    mine = jnp.full(group_codes.shape[2:], -1, jnp.int32)
    for s in range(groups):
        mine = jnp.where(lanes == s, jnp.broadcast_to(in_codes[s, 0:1, :], mine.shape), mine)
    group_codes[0, 0] = mine
    for t in range(1, inner):
        send(group_codes.at[0, 0], group_codes.at[0, t], sem_xcode, (t - 1,), x_dev(t))
    keep(group_codes.at[0, 0], code_out, 0)

    @pl.loop(0, WIDTH // 256)
    def _(i):
        ids = lax.broadcasted_iota(jnp.int32, (256, cap), 0) + i * 256
        for s in range(groups):
            hit = ids == in_codes[s, 0:1, :]
            member[pl.ds(pl.multiple_of(i * 256, 256), 256), s * cap : (s + 1) * cap] = jnp.where(
                hit, 1.0, 0.0
            ).astype(jnp.bfloat16)

    def add_up(q, r):
        if r == 0:
            for t in order:
                s = (g - t + groups) % groups
                remote(
                    arrived.at[q, s], arrived.at[q, s], sem_vec, (q, t - 1), {"grp": grp_at(t)}
                ).wait_recv()
            keep(arrived.at[q], arr_out.at[q], 2 + q)
        for t in [*range(1, inner), 0]:
            xt = (xi + t) % inner
            total = jnp.dot(
                member[pl.ds(pl.multiple_of(xt * share + r * tall, tall), tall), :],
                arrived[q].reshape(slots, cols),
                preferred_element_type=jnp.float32,
            )
            sums[q, r, xt] = total.astype(jnp.bfloat16)
            if t:
                send(sums.at[q, r, xt], x_in.at[q, r, t - 1], sem_x, (q, r, t - 1), x_dev(t))

    def over_x(q, r):
        for t in range(1, inner):
            remote(x_in.at[q, r, t - 1], x_in.at[q, r, t - 1], sem_x, (q, r, t - 1), x_dev(t)).wait_recv()
        for near in (True, False):
            which = 1 - side if near else side
            for duo_to in range(duos):
                zt = 2 * duo_to + which
                span = pl.ds(pl.multiple_of(zt * part, part), part)
                total = sums[q, r, xi, span, :].astype(jnp.float32)
                for u in range(inner - 1):
                    total = total + x_in[q, r, u, span, :].astype(jnp.float32)
                half[q, r, which, duo_to] = total.astype(jnp.bfloat16)
            if near:
                send(half.at[q, r, which], z_near.at[q, r], sem_z, (q, r, 0), at_z(next_z))

    def near_z(q, r):
        remote(z_near.at[q, r], z_near.at[q, r], sem_z, (q, r, 0), at_z(next_z)).wait_recv()
        for t in range(1, duos):
            to = (duo + t) % duos
            total = half[q, r, side, to].astype(jnp.float32) + z_near[q, r, to].astype(jnp.float32)
            pair[q, r, t - 1] = total.astype(jnp.bfloat16)
            send(pair.at[q, r, t - 1], z_far.at[q, r, t - 1], sem_z, (q, r, t), at_z(far_z(t)))

    def codes_over_x():
        for t in range(1, inner):
            remote(group_codes.at[0, t], group_codes.at[0, t], sem_xcode, (t - 1,), x_dev(t)).wait_recv()
        for t in range(1, outer):
            send(group_codes.at[0], group_codes.at[t], sem_zcode, (t - 1,), z_dev(t))

    def codes_over_z():
        for t in range(1, outer):
            remote(group_codes.at[t], group_codes.at[t], sem_zcode, (t - 1,), z_dev(t)).wait_recv()

    def count_children(r):
        ids = lax.broadcasted_iota(jnp.int32, (part, 128), 0) + ((xi * PIECES + r) * outer + zi) * part

        def one_member(i, running):
            block = group_codes.at[i // inner, i % inner]
            for s in range(groups):
                for lane in range(0, cap, 128):
                    hit = ids == block[s : s + 1, lane : lane + 128]
                    running = running + jnp.where(hit, 1.0, 0.0)
            return running

        tally = lax.fori_loop(0, inner * outer, one_member, jnp.zeros((part, 128), jnp.float32))
        return jnp.maximum(jnp.sum(tally, axis=1, keepdims=True), 1.0)

    def over_z(q, r):
        for t in range(1, duos):
            remote(
                z_far.at[q, r, t - 1], z_far.at[q, r, t - 1], sem_z, (q, r, t), at_z(far_z(t))
            ).wait_recv()
        total = half[q, r, side, duo].astype(jnp.float32) + z_near[q, r, duo].astype(jnp.float32)
        for u in range(duos - 1):
            total = total + z_far[q, r, u].astype(jnp.float32)
        cent[q, xi, r, zi] = (total / tallies[r]).astype(jnp.bfloat16)
        block = cent.at[q, xi, r, zi]
        for t in range(1, duos):
            send(block, block, sem_zc, (q, r, t), at_z(far_z(t)))
        send(block, block, sem_zc, (q, r, 0), at_z(next_z))
        for u in range(1, inner):
            send(block, block, sem_xc, (q, r, 0, u - 1), x_dev(u))

    def from_z(q, r, z, number, relay):
        block = cent.at[q, xi, r, z]
        remote(block, block, sem_zc, (q, r, number), at_z(next_z)).wait_recv()
        if relay:
            send(block, block, sem_zc, (q, r, duos + number - 1), at_z(next_z))
        for u in range(1, inner):
            send(block, block, sem_xc, (q, r, number + 1, u - 1), x_dev(u))

    def back_over_z(q, r):
        from_z(q, r, next_z, 0, False)
        for t in range(1, duos):
            from_z(q, r, 2 * ((duo - t + duos) % duos) + side, t, True)

    def back_near(q, r):
        for t in range(1, duos):
            from_z(q, r, 2 * ((duo - t + duos) % duos) + 1 - side, duos + t - 1, False)

    behind = [2 * ((duo - t + duos) % duos) for t in range(1, duos)]
    origins = [zi, next_z, *(z + side for z in behind), *(z + 1 - side for z in behind)]

    def back_over_x(q, r):
        for t in range(outer):
            for u in range(1, inner):
                block = cent.at[q, (xi - u + inner) % inner, r, origins[t]]
                remote(block, block, sem_xc, (q, r, t, u - 1), x_dev(u)).wait_recv()
        for x in range(inner):
            keep(cent.at[q, x, r], cent_out.at[q, x, r], 2 + blocks + (q * PIECES + r) * inner + x)
        for x in range(inner):
            for base in range(0, tall, 128):
                wide = cent[q, x, r].reshape(tall, cols)[base : base + 128].astype(jnp.float32)
                wide = wide * wide
                square = wide[:, 0:128]
                for lane in range(128, cols, 128):
                    square = square + wide[:, lane : lane + 128]
                child = (x * PIECES + r) * tall + base
                if q > 0:
                    square = square + squares[child : child + 128, :]
                if q < blocks - 1:
                    squares[child : child + 128, :] = square
                else:
                    norms[:, child : child + 128] = jnp.broadcast_to(
                        jnp.sum(square.T, axis=0, keepdims=True), (8, 128)
                    )

    tasks = []
    for q in range(blocks):
        for r in range(PIECES):
            sum_at = 22.0 * q + r
            x_at = 22.0 * q + 12.0 + 11.0 * r
            stages = (add_up, over_x, near_z, over_z, back_over_z, back_near, back_over_x)
            for number, stage in enumerate(stages):
                when = sum_at if number == 0 else x_at + 9.0 * (number - 1)
                tasks.append((when / 2.0, number, stage, (q, r)))
    tasks.append((1.5, 9, codes_over_x, ()))
    tasks.append((8.5, 9, codes_over_z, ()))
    tallies = []
    for r in range(PIECES):
        tasks.append((8.6 + r / 10, 9, lambda number: tallies.append(count_children(number)), (r,)))
    for when, number, stage, where in sorted(tasks, key=lambda task: task[:2]):
        stage(*where)

    keep(norms, norm_out, 1)
    for copy in kept:
        copy.wait()
    for copy in sent:
        copy.wait_send()


def distance_kernel(depth, arr_ref, cent_ref, code_ref, norm_ref, out_ref):
    blocks, rows = arr_ref.shape[:2]
    mark = pl.program_id(0)
    lanes = lax.broadcasted_iota(jnp.int32, code_ref.shape, 0)
    row_codes = jnp.sum(jnp.where(lanes == mark, code_ref[...], 0), axis=0, keepdims=True)
    column = jnp.broadcast_to(row_codes.astype(jnp.float32), (128, rows)).T[:, 0:1]
    x = jnp.concatenate([arr_ref[q] for q in range(blocks)], axis=1)
    wide = x.astype(jnp.float32)
    second = column >= CHILD
    filled = column >= 0
    x_norm = jnp.sum(wide * wide, axis=1, keepdims=True) * (1.0 / depth)
    step = 256
    for base in range(0, CHILD, step):
        crosses, squares = [], []
        for p in range(PAR_GRP):
            start = p * CHILD + base
            c = jnp.concatenate([cent_ref[q, start : start + step, :] for q in range(blocks)], axis=1)
            crosses.append(
                lax.dot_general(x, c, (((1,), (1,)), ((), ())), preferred_element_type=jnp.float32)
            )
            squares.append(norm_ref[0:1, start : start + step] * (1.0 / depth))
        cross = jnp.where(second, crosses[1], crosses[0])
        square = jnp.where(second, squares[1], squares[0])
        dist = (x_norm + square) - cross * (2.0 / depth)
        out_ref[:, base : base + step] = jnp.where(filled, dist, 0.0)


def body(vectors, parents, children, counts):
    groups = lax.axis_size("grp")
    members = lax.axis_size("mem")
    inner = inner_size(members)
    outer = members // inner
    rows, depth = vectors.shape
    cap = 2 * rows // groups
    slots = groups * cap
    cols = 256
    blocks = depth // cols
    share = WIDTH // inner
    tall = share // PIECES
    part = tall // outer
    code_high = max(8, groups)
    bf16, i32 = jnp.bfloat16, jnp.int32
    dims = (groups, inner, outer, rows, cap, blocks, cols)
    vmem = pltpu.VMEM
    dma = pltpu.SemaphoreType.DMA
    arr, cent, codes, norms = pl.pallas_call(
        functools.partial(exchange_kernel, dims),
        out_shape=(
            jax.ShapeDtypeStruct((blocks, groups, cap, cols), bf16),
            jax.ShapeDtypeStruct((blocks, inner, PIECES, outer, part, cols), bf16),
            jax.ShapeDtypeStruct((code_high, cap), i32),
            jax.ShapeDtypeStruct((8, WIDTH), jnp.float32),
        ),
        in_specs=[
            pl.BlockSpec(memory_space=pltpu.SMEM),
            pl.BlockSpec(memory_space=vmem),
            pl.BlockSpec(memory_space=vmem),
            pl.BlockSpec(memory_space=vmem),
        ],
        out_specs=(pl.BlockSpec(memory_space=pl.ANY),) * 4,
        scratch_shapes=[
            vmem((groups, cap, rows), bf16),
            vmem((groups - 1, 8, cap), i32),
            vmem((groups, 8, cap), i32),
            vmem((outer, inner, code_high, cap), i32),
            vmem((blocks, groups - 1, cap, cols), bf16),
            vmem((blocks, groups, cap, cols), bf16),
            vmem((WIDTH, slots), bf16),
            vmem((blocks, PIECES, inner, tall, cols), bf16),
            vmem((blocks, PIECES, inner - 1, tall, cols), bf16),
            vmem((blocks, PIECES, 2, outer // 2, part, cols), bf16),
            vmem((blocks, PIECES, outer // 2, part, cols), bf16),
            vmem((blocks, PIECES, outer // 2 - 1, part, cols), bf16),
            vmem((blocks, PIECES, outer // 2 - 1, part, cols), bf16),
            vmem((blocks, inner, PIECES, outer, part, cols), bf16),
            vmem((WIDTH, 128), jnp.float32),
            vmem((8, WIDTH), jnp.float32),
            dma((2, groups - 1)),
            dma((2, blocks, groups - 1)),
            dma((2, inner - 1)),
            dma((2, outer - 1)),
            dma((2, blocks, PIECES, inner - 1)),
            dma((2, blocks, PIECES, outer - 1)),
            dma((2, blocks, PIECES, outer - 1)),
            dma((2, blocks, PIECES, outer, inner - 1)),
            dma((2 + blocks + blocks * PIECES * inner,)),
        ],
        compiler_params=pltpu.CompilerParams(
            collective_id=0, has_side_effects=True, vmem_limit_bytes=56 * MIB
        ),
    )(counts, vectors, parents.reshape(1, rows), children.reshape(1, rows))
    arr = arr.reshape(blocks, slots, cols)
    cent = cent.reshape(blocks, WIDTH, cols)
    return pl.pallas_call(
        functools.partial(distance_kernel, depth),
        grid=(groups,),
        out_shape=jax.ShapeDtypeStruct((slots, CHILD), jnp.float32),
        in_specs=[
            pl.BlockSpec((blocks, cap, cols), lambda i: (0, i, 0)),
            pl.BlockSpec((blocks, WIDTH, cols), lambda i: (0, 0, 0)),
            pl.BlockSpec((code_high, cap), lambda i: (0, 0)),
            pl.BlockSpec((8, WIDTH), lambda i: (0, 0)),
        ],
        out_specs=pl.BlockSpec((cap, CHILD), lambda i: (i, 0)),
        compiler_params=pltpu.CompilerParams(vmem_limit_bytes=60 * MIB),
    )(arr, cent, codes, norms)


def solution(mesh):
    in_specs = (
        P(("grp", "mem"), None),
        P(("grp", "mem")),
        P(("grp", "mem")),
        P(("grp", "mem"), None),
    )
    out_specs = P(("grp", "mem"), None)
    return jax.shard_map(body, mesh=mesh, in_specs=in_specs, out_specs=out_specs, check_vma=False)
```

```python
import functools

import jax
import jax.numpy as jnp
from jax import lax
from jax.experimental import pallas as pl
from jax.experimental.pallas import tpu as pltpu
from jax.sharding import PartitionSpec as P

CHILD = 1024
PAR_GRP = 2
WIDTH = PAR_GRP * CHILD
LOW = 32
MIB = 1024 * 1024
PIECES = 4
TOGETHER = 2


def inner_size(members):
    return max(d for d in range(1, members + 1) if members % d == 0 and d * d <= members)


def exchange_kernel(
    dims,
    counts_ref,
    vec_ref,
    par_ref,
    chi_ref,
    arr_out,
    cent_out,
    code_out,
    norm_out,
    pick,
    out_codes,
    in_codes,
    group_codes,
    outgoing,
    arrived,
    member,
    sums,
    x_in,
    half,
    z_near,
    pair,
    z_far,
    cent,
    squares,
    norms,
    sem_code,
    sem_vec,
    sem_xcode,
    sem_zcode,
    sem_x,
    sem_z,
    sem_zc,
    sem_xc,
    sem_local,
):
    groups, inner, outer, rows, cap, blocks, cols = dims
    slots = groups * cap
    share = WIDTH // inner
    tall = share // PIECES
    part = tall // outer
    g = lax.axis_index("grp")
    m = lax.axis_index("mem")
    zi, xi = m // inner, m % inner
    duos = outer // 2
    side, duo = zi % 2, zi // 2
    next_z = zi + 1 - 2 * side

    def far_z(t):
        return 2 * ((duo + t) % duos) + side

    def grp_at(t):
        return (g + t) % groups

    def x_dev(t):
        return {"mem": zi * inner + (xi + t) % inner}

    def z_dev(t):
        return {"mem": ((zi + t) % outer) * inner + xi}

    def at_z(z):
        return {"mem": z * inner + xi}

    barrier = pltpu.get_barrier_semaphore()
    for t in range(1, groups):
        pl.semaphore_signal(barrier, inc=1, device_id={"grp": grp_at(t)}, device_id_type=pl.DeviceIdType.MESH)
    for t in range(1, inner):
        pl.semaphore_signal(barrier, inc=1, device_id=x_dev(t), device_id_type=pl.DeviceIdType.MESH)
    for t in range(1, outer):
        pl.semaphore_signal(barrier, inc=1, device_id=z_dev(t), device_id_type=pl.DeviceIdType.MESH)

    def remote(src, dst, sems, where, device):
        return pltpu.make_async_remote_copy(
            src_ref=src,
            dst_ref=dst,
            send_sem=sems.at[(0,) + where],
            recv_sem=sems.at[(1,) + where],
            device_id=device,
            device_id_type=pl.DeviceIdType.MESH,
        )

    sent = []
    kept = []

    def send(*what):
        copy = remote(*what)
        copy.start()
        sent.append(copy)

    def keep(src, dst, number):
        copy = pltpu.make_async_copy(src, dst, sem_local.at[number])
        copy.start()
        kept.append(copy)

    code = par_ref[...] * CHILD + chi_ref[...]
    high = (code // LOW + 1).astype(jnp.float32)
    low = (code % LOW).astype(jnp.float32)
    first = lax.broadcasted_iota(jnp.int32, (16, rows), 0) == 0
    code_rows = jnp.where(first, high, low).astype(jnp.bfloat16)
    step = min(cap, 256)

    def make_pick(t):
        h = grp_at(t)
        count = counts_ref[0, h]
        offset = jnp.int32(0)
        for other in range(groups):
            offset = offset + jnp.where(other < h, counts_ref[0, other], 0)
        for base in range(0, cap, step):
            slot = lax.broadcasted_iota(jnp.int32, (step, rows), 0) + base
            row = lax.broadcasted_iota(jnp.int32, (step, rows), 1)
            chosen = jnp.logical_and(row - slot == offset, slot < count)
            pick[t, base : base + step, :] = jnp.where(chosen, 1.0, 0.0).astype(jnp.bfloat16)
        got = lax.dot_general(
            code_rows, pick[t], (((1,), (1,)), ((), ())), preferred_element_type=jnp.float32
        )
        value = (got[0:1] * LOW + got[1:2] - LOW).astype(jnp.int32)
        return jnp.broadcast_to(value, (8, cap))

    def picked(t, q):
        return jnp.dot(
            pick[t], vec_ref[:, q * cols : (q + 1) * cols], preferred_element_type=jnp.float32
        ).astype(jnp.bfloat16)

    def send_rows(t, q):
        outgoing[q, t - 1] = picked(t, q)
        send(outgoing.at[q, t - 1], arrived.at[q, g], sem_vec, (q, t - 1), {"grp": grp_at(t)})

    order = sorted(range(1, groups), key=lambda t: abs(2 * t - groups))
    for place, t in enumerate(order):
        out_codes[t - 1] = make_pick(t)
        outgoing[0, t - 1] = picked(t, 0)
        if place == 0:
            pl.semaphore_wait(barrier, groups + inner + outer - 3)
        send(out_codes.at[t - 1], in_codes.at[g], sem_code, (t - 1,), {"grp": grp_at(t)})
        send(outgoing.at[0, t - 1], arrived.at[0, g], sem_vec, (0, t - 1), {"grp": grp_at(t)})
    in_codes[g] = make_pick(0)
    arrived[0, g] = picked(0, 0)
    for q in range(1, blocks):
        for t in order:
            send_rows(t, q)
        arrived[q, g] = picked(0, q)

    for t in order:
        s = (g - t + groups) % groups
        remote(in_codes.at[s], in_codes.at[s], sem_code, (t - 1,), {"grp": grp_at(t)}).wait_recv()
    lanes = lax.broadcasted_iota(jnp.int32, group_codes.shape[2:], 0)
    mine = jnp.full(group_codes.shape[2:], -1, jnp.int32)
    for s in range(groups):
        mine = jnp.where(lanes == s, jnp.broadcast_to(in_codes[s, 0:1, :], mine.shape), mine)
    group_codes[0, 0] = mine
    for t in range(1, inner):
        send(group_codes.at[0, 0], group_codes.at[0, t], sem_xcode, (t - 1,), x_dev(t))
    keep(group_codes.at[0, 0], code_out, 0)

    @pl.loop(0, WIDTH // 256)
    def _(i):
        ids = lax.broadcasted_iota(jnp.int32, (256, cap), 0) + i * 256
        for s in range(groups):
            hit = ids == in_codes[s, 0:1, :]
            member[pl.ds(pl.multiple_of(i * 256, 256), 256), s * cap : (s + 1) * cap] = jnp.where(
                hit, 1.0, 0.0
            ).astype(jnp.bfloat16)

    def add_up(q, r):
        if r == 0:
            for t in order:
                s = (g - t + groups) % groups
                remote(
                    arrived.at[q, s], arrived.at[q, s], sem_vec, (q, t - 1), {"grp": grp_at(t)}
                ).wait_recv()
            keep(arrived.at[q], arr_out.at[q], 2 + q)
        for t in [*range(1, inner), 0]:
            xt = (xi + t) % inner
            total = jnp.dot(
                member[pl.ds(pl.multiple_of(xt * share + r * tall, tall), TOGETHER * tall), :],
                arrived[q].reshape(slots, cols),
                preferred_element_type=jnp.float32,
            ).astype(jnp.bfloat16)
            for place in range(TOGETHER):
                at = r + place
                sums[q, at, xt] = total[place * tall : (place + 1) * tall]
                if t:
                    send(sums.at[q, at, xt], x_in.at[q, at, t - 1], sem_x, (q, at, t - 1), x_dev(t))

    def over_x(q, r):
        for t in range(1, inner):
            remote(x_in.at[q, r, t - 1], x_in.at[q, r, t - 1], sem_x, (q, r, t - 1), x_dev(t)).wait_recv()
        for near in (True, False):
            which = 1 - side if near else side
            for duo_to in range(duos):
                zt = 2 * duo_to + which
                span = pl.ds(pl.multiple_of(zt * part, part), part)
                total = sums[q, r, xi, span, :].astype(jnp.float32)
                for u in range(inner - 1):
                    total = total + x_in[q, r, u, span, :].astype(jnp.float32)
                half[q, r, which, duo_to] = total.astype(jnp.bfloat16)
            if near:
                send(half.at[q, r, which], z_near.at[q, r], sem_z, (q, r, 0), at_z(next_z))

    def near_z(q, r):
        remote(z_near.at[q, r], z_near.at[q, r], sem_z, (q, r, 0), at_z(next_z)).wait_recv()
        for t in range(1, duos):
            to = (duo + t) % duos
            total = half[q, r, side, to].astype(jnp.float32) + z_near[q, r, to].astype(jnp.float32)
            pair[q, r, t - 1] = total.astype(jnp.bfloat16)
            send(pair.at[q, r, t - 1], z_far.at[q, r, t - 1], sem_z, (q, r, t), at_z(far_z(t)))

    def codes_over_x():
        for t in range(1, inner):
            remote(group_codes.at[0, t], group_codes.at[0, t], sem_xcode, (t - 1,), x_dev(t)).wait_recv()
        for t in range(1, outer):
            send(group_codes.at[0], group_codes.at[t], sem_zcode, (t - 1,), z_dev(t))

    def codes_over_z():
        for t in range(1, outer):
            remote(group_codes.at[t], group_codes.at[t], sem_zcode, (t - 1,), z_dev(t)).wait_recv()

    def count_children(r):
        ids = lax.broadcasted_iota(jnp.int32, (part, 128), 0) + ((xi * PIECES + r) * outer + zi) * part

        def one_member(i, running):
            block = group_codes.at[i // inner, i % inner]
            for s in range(groups):
                for lane in range(0, cap, 128):
                    hit = ids == block[s : s + 1, lane : lane + 128]
                    running = running + jnp.where(hit, 1.0, 0.0)
            return running

        tally = lax.fori_loop(0, inner * outer, one_member, jnp.zeros((part, 128), jnp.float32))
        return jnp.maximum(jnp.sum(tally, axis=1, keepdims=True), 1.0)

    def over_z(q, r):
        for t in range(1, duos):
            remote(
                z_far.at[q, r, t - 1], z_far.at[q, r, t - 1], sem_z, (q, r, t), at_z(far_z(t))
            ).wait_recv()
        total = half[q, r, side, duo].astype(jnp.float32) + z_near[q, r, duo].astype(jnp.float32)
        for u in range(duos - 1):
            total = total + z_far[q, r, u].astype(jnp.float32)
        cent[q, xi, r, zi] = (total / tallies[r]).astype(jnp.bfloat16)
        block = cent.at[q, xi, r, zi]
        for t in range(1, duos):
            send(block, block, sem_zc, (q, r, t), at_z(far_z(t)))
        send(block, block, sem_zc, (q, r, 0), at_z(next_z))
        for u in range(1, inner):
            send(block, block, sem_xc, (q, r, 0, u - 1), x_dev(u))

    def from_z(q, r, z, number, relay):
        block = cent.at[q, xi, r, z]
        remote(block, block, sem_zc, (q, r, number), at_z(next_z)).wait_recv()
        if relay:
            send(block, block, sem_zc, (q, r, duos + number - 1), at_z(next_z))
        for u in range(1, inner):
            send(block, block, sem_xc, (q, r, number + 1, u - 1), x_dev(u))

    def back_over_z(q, r):
        from_z(q, r, next_z, 0, False)
        for t in range(1, duos):
            from_z(q, r, 2 * ((duo - t + duos) % duos) + side, t, True)

    def back_near(q, r):
        for t in range(1, duos):
            from_z(q, r, 2 * ((duo - t + duos) % duos) + 1 - side, duos + t - 1, False)

    behind = [2 * ((duo - t + duos) % duos) for t in range(1, duos)]
    origins = [zi, next_z, *(z + side for z in behind), *(z + 1 - side for z in behind)]

    def back_over_x(q, r):
        for t in range(outer):
            for u in range(1, inner):
                block = cent.at[q, (xi - u + inner) % inner, r, origins[t]]
                remote(block, block, sem_xc, (q, r, t, u - 1), x_dev(u)).wait_recv()
        for x in range(inner):
            keep(cent.at[q, x, r], cent_out.at[q, x, r], 2 + blocks + (q * PIECES + r) * inner + x)
        for x in range(inner):
            for base in range(0, tall, 128):
                wide = cent[q, x, r].reshape(tall, cols)[base : base + 128].astype(jnp.float32)
                wide = wide * wide
                square = wide[:, 0:128]
                for lane in range(128, cols, 128):
                    square = square + wide[:, lane : lane + 128]
                child = (x * PIECES + r) * tall + base
                if q > 0:
                    square = square + squares[child : child + 128, :]
                if q < blocks - 1:
                    squares[child : child + 128, :] = square
                else:
                    norms[:, child : child + 128] = jnp.broadcast_to(
                        jnp.sum(square.T, axis=0, keepdims=True), (8, 128)
                    )

    tasks = []
    for q in range(blocks):
        for r in range(PIECES):
            sum_at = 22.0 * q + r
            x_at = 22.0 * q + 7.0 + 6.0 * r
            stages = (add_up, over_x, near_z, over_z, back_over_z, back_near, back_over_x)
            for number, stage in enumerate(stages):
                when = sum_at if number == 0 else x_at + 6.0 * (number - 1)
                if number or r % TOGETHER == 0:
                    tasks.append((when / 2.0, number, stage, (q, r)))
    tasks.append((1.5, 9, codes_over_x, ()))
    tasks.append((7.5, 9, codes_over_z, ()))
    tallies = []
    for r in range(PIECES):
        tasks.append((7.6 + r / 10, 9, lambda number: tallies.append(count_children(number)), (r,)))
    for when, number, stage, where in sorted(tasks, key=lambda task: task[:2]):
        stage(*where)

    keep(norms, norm_out, 1)
    for copy in kept:
        copy.wait()
    for copy in sent:
        copy.wait_send()


def distance_kernel(depth, arr_ref, cent_ref, code_ref, norm_ref, out_ref):
    blocks, rows = arr_ref.shape[:2]
    mark = pl.program_id(0)
    lanes = lax.broadcasted_iota(jnp.int32, code_ref.shape, 0)
    row_codes = jnp.sum(jnp.where(lanes == mark, code_ref[...], 0), axis=0, keepdims=True)
    column = jnp.broadcast_to(row_codes.astype(jnp.float32), (128, rows)).T[:, 0:1]
    x = jnp.concatenate([arr_ref[q] for q in range(blocks)], axis=1)
    wide = x.astype(jnp.float32)
    second = column >= CHILD
    filled = column >= 0
    x_norm = jnp.sum(wide * wide, axis=1, keepdims=True) * (1.0 / depth)
    step = 256
    for base in range(0, CHILD, step):
        crosses, squares = [], []
        for p in range(PAR_GRP):
            start = p * CHILD + base
            c = jnp.concatenate([cent_ref[q, start : start + step, :] for q in range(blocks)], axis=1)
            crosses.append(
                lax.dot_general(x, c, (((1,), (1,)), ((), ())), preferred_element_type=jnp.float32)
            )
            squares.append(norm_ref[0:1, start : start + step] * (1.0 / depth))
        cross = jnp.where(second, crosses[1], crosses[0])
        square = jnp.where(second, squares[1], squares[0])
        dist = (x_norm + square) - cross * (2.0 / depth)
        out_ref[:, base : base + step] = jnp.where(filled, dist, 0.0)


def body(vectors, parents, children, counts):
    groups = lax.axis_size("grp")
    members = lax.axis_size("mem")
    inner = inner_size(members)
    outer = members // inner
    rows, depth = vectors.shape
    cap = 2 * rows // groups
    slots = groups * cap
    cols = 256
    blocks = depth // cols
    share = WIDTH // inner
    tall = share // PIECES
    part = tall // outer
    code_high = max(8, groups)
    bf16, i32 = jnp.bfloat16, jnp.int32
    dims = (groups, inner, outer, rows, cap, blocks, cols)
    vmem = pltpu.VMEM
    dma = pltpu.SemaphoreType.DMA
    arr, cent, codes, norms = pl.pallas_call(
        functools.partial(exchange_kernel, dims),
        out_shape=(
            jax.ShapeDtypeStruct((blocks, groups, cap, cols), bf16),
            jax.ShapeDtypeStruct((blocks, inner, PIECES, outer, part, cols), bf16),
            jax.ShapeDtypeStruct((code_high, cap), i32),
            jax.ShapeDtypeStruct((8, WIDTH), jnp.float32),
        ),
        in_specs=[
            pl.BlockSpec(memory_space=pltpu.SMEM),
            pl.BlockSpec(memory_space=vmem),
            pl.BlockSpec(memory_space=vmem),
            pl.BlockSpec(memory_space=vmem),
        ],
        out_specs=(pl.BlockSpec(memory_space=pl.ANY),) * 4,
        scratch_shapes=[
            vmem((groups, cap, rows), bf16),
            vmem((groups - 1, 8, cap), i32),
            vmem((groups, 8, cap), i32),
            vmem((outer, inner, code_high, cap), i32),
            vmem((blocks, groups - 1, cap, cols), bf16),
            vmem((blocks, groups, cap, cols), bf16),
            vmem((WIDTH, slots), bf16),
            vmem((blocks, PIECES, inner, tall, cols), bf16),
            vmem((blocks, PIECES, inner - 1, tall, cols), bf16),
            vmem((blocks, PIECES, 2, outer // 2, part, cols), bf16),
            vmem((blocks, PIECES, outer // 2, part, cols), bf16),
            vmem((blocks, PIECES, outer // 2 - 1, part, cols), bf16),
            vmem((blocks, PIECES, outer // 2 - 1, part, cols), bf16),
            vmem((blocks, inner, PIECES, outer, part, cols), bf16),
            vmem((WIDTH, 128), jnp.float32),
            vmem((8, WIDTH), jnp.float32),
            dma((2, groups - 1)),
            dma((2, blocks, groups - 1)),
            dma((2, inner - 1)),
            dma((2, outer - 1)),
            dma((2, blocks, PIECES, inner - 1)),
            dma((2, blocks, PIECES, outer - 1)),
            dma((2, blocks, PIECES, outer - 1)),
            dma((2, blocks, PIECES, outer, inner - 1)),
            dma((2 + blocks + blocks * PIECES * inner,)),
        ],
        compiler_params=pltpu.CompilerParams(
            collective_id=0, has_side_effects=True, vmem_limit_bytes=56 * MIB
        ),
    )(counts, vectors, parents.reshape(1, rows), children.reshape(1, rows))
    arr = arr.reshape(blocks, slots, cols)
    cent = cent.reshape(blocks, WIDTH, cols)
    return pl.pallas_call(
        functools.partial(distance_kernel, depth),
        grid=(groups,),
        out_shape=jax.ShapeDtypeStruct((slots, CHILD), jnp.float32),
        in_specs=[
            pl.BlockSpec((blocks, cap, cols), lambda i: (0, i, 0)),
            pl.BlockSpec((blocks, WIDTH, cols), lambda i: (0, 0, 0)),
            pl.BlockSpec((code_high, cap), lambda i: (0, 0)),
            pl.BlockSpec((8, WIDTH), lambda i: (0, 0)),
        ],
        out_specs=pl.BlockSpec((cap, CHILD), lambda i: (i, 0)),
        compiler_params=pltpu.CompilerParams(vmem_limit_bytes=60 * MIB),
    )(arr, cent, codes, norms)


def solution(mesh):
    in_specs = (
        P(("grp", "mem"), None),
        P(("grp", "mem")),
        P(("grp", "mem")),
        P(("grp", "mem"), None),
    )
    out_specs = P(("grp", "mem"), None)
    return jax.shard_map(body, mesh=mesh, in_specs=in_specs, out_specs=out_specs, check_vma=False)
```
